256 devices in a mesh: inst: 32 (over x, z_hi, core), head: 8 (over y, z_lo).
Axes of the slice: x: 4, y: 4, z: 8 (z_hi: 4, z_lo: 2; z = z_hi * 2 + z_lo), core: 2. Of those that a mesh axis runs over, the one named last changes fastest.
Arguments:
- kv_cache: bfloat16 [768, 2, 128, 512], P('inst', None, None, 'head'), may hold values from -5 to 5
- query: bfloat16 [768, 8192], P('inst', 'head'), may hold values from -120 to 120
- fresh_kv: bfloat16 [768, 1024], P('inst', 'head'), may hold values from -5 to 5
- lengths: int32 [768], replicated, may hold values from 1 to 128, 49152 in all
- owner: int32 [768, 1], replicated, may hold values from 0 to 31; in each aligned block of 24 rows (0 to 23, 24 to 47, ...) at most 2 rows name the same one
- tokens: bfloat16 [4096, 4096], P(('inst', 'head')), may hold values from -6 to 6
- expert_ids: int32 [4096, 8], P(('inst', 'head')), may hold values from 0 to 127, all different within a row; in each aligned block of 16 rows (0 to 15, 16 to 31, ...) at most 2 rows name the same one
- gate_weights: float32 [4096, 8], P(('inst', 'head')), may hold values from 0.1 to 0.5
- w_gate: bfloat16 [98304, 4096], P(('inst', 'head')), may hold values from -0.09375 to 0.09375
- w_up: bfloat16 [98304, 4096], P(('inst', 'head')), may hold values from -0.09375 to 0.09375
- w_down: bfloat16 [98304, 4096], P(('inst', 'head')), may hold values from -0.21875 to 0.21875
Outputs:
- handed_cache: bfloat16 [2048, 2, 128, 512], P(('inst', 'head'))
- attention: bfloat16 [2048, 8192], P(('inst', 'head'))
- moe_out: bfloat16 [4096, 4096], P(('inst', 'head'))
The draws below stay inside these ranges and needn't reach their ends.
Inputs may be any that keep to these rules, and one draw needn't show every extreme that they name: `owner`: in each aligned block of 24 prompts no decode instance is named more than 2 times, and some decode instance exactly 2 times. `expert_ids`: each row names 8 different experts; among the rows of one device (aligned blocks of 16 rows) no expert is named more than 2 times, a bound that some block reaches.
All inputs are finite; a program needn't handle non-finite values.
Results may differ from the reference program's by a relative error of at most 0.015.
Values may be sent and summed in bfloat16 or wider, within the bound.
A program may use at most 128 MiB of HBM per device.

```python
import math
import jax
import jax.numpy as jnp
import numpy as np
from jax import lax

D = 4096
QUERY_HEADS = 64
KEY_VALUE_HEADS = 4
HEAD_DIM_SIZE = 128
FFE = 768
TOP = 8
EXP_INST = 4
P_DEV = 24
CACHE_POSITIONS = 128
M_DEV = 16
EXPERTS = 128
PROMPT_TOTAL = 768
CAP = 2
CAPE = 2
MTOK = 4096
N_INST = 32
N_HEAD = 8


def anchor_keys(key):
    starting_keys = jax.random.normal(jax.random.fold_in(key, 901), (PROMPT_TOTAL, KEY_VALUE_HEADS * HEAD_DIM_SIZE), jnp.float32)
    return jnp.clip(starting_keys, -4.0, 4.0)


def draw_kv_cache(key, part):
    anchor_point = anchor_keys(key)
    key = jax.random.fold_in(key, 11)
    every_value = jnp.clip(jax.random.normal(key, (PROMPT_TOTAL, 2, CACHE_POSITIONS, KEY_VALUE_HEADS * HEAD_DIM_SIZE), jnp.float32), -5.0, 5.0)
    every_value = every_value.at[:, 0, 0, :].set(anchor_point)
    return every_value.astype(jnp.bfloat16)


def draw_query(key, part):
    key = jax.random.fold_in(key, 12)
    every_value = jnp.clip(jax.random.normal(key, (PROMPT_TOTAL, QUERY_HEADS, HEAD_DIM_SIZE), jnp.float32), -5.0, 5.0)
    return every_value.reshape(PROMPT_TOTAL, QUERY_HEADS * HEAD_DIM_SIZE).astype(jnp.bfloat16)


def draw_fresh_kv(key, part):
    key = jax.random.fold_in(key, 13)
    every_value = jnp.clip(jax.random.normal(key, (PROMPT_TOTAL, 2 * KEY_VALUE_HEADS * HEAD_DIM_SIZE), jnp.float32), -5.0, 5.0)
    return every_value.astype(jnp.bfloat16)


def shard_levels(rng, extent, shards, smallest, high):
    factor_of, own = 1.0, jax.random.fold_in(rng, 6)
    for position, shards_of in shards:
        draws = jnp.exp(jax.random.uniform(jax.random.fold_in(own, position), (shards_of,), jnp.float32, smallest / len(shards), high / len(shards)))
        factor_of = factor_of * jnp.repeat(draws, extent[position] // shards_of).reshape([-1 if axis == position else 1 for axis in range(len(extent))])
    return factor_of


def length_profile(amount, total, limit, skew):
    portions = [(1 << 20) // math.isqrt(grade ** skew) + 1 for grade in range(2, amount + 1)]
    surplus, holding = total - limit - (amount - 1), [1] * (amount - 1)
    while surplus > 0:
        movable = [i for i in range(amount - 1) if holding[i] < limit]
        pool, remaining = sum([portions[i] for i in movable]), surplus
        for i in movable:
            addition = min(limit - holding[i], max(1, remaining * portions[i] // pool), surplus)
            holding[i] = holding[i] + addition
            surplus = surplus - addition
    return np.array([limit] + holding)


def uneven_parts(key, number_of, total, most, skew):
    if number_of == 2:
        one = jax.random.randint(key, (), max(1, total - most), min(most, total - 1) + 1)
        return jnp.stack([one, total - one])
    sizes = jnp.asarray(length_profile(number_of, total, most, skew), jnp.int32)
    pairs = (number_of - 1) // 2
    donor, receiver = sizes[1:1 + 2 * pairs:2], sizes[2:2 + 2 * pairs:2]
    margin = jnp.minimum(donor - 1, most - receiver)
    moved = jax.random.randint(jax.random.fold_in(key, 1), (pairs,), 0, 1 << 20) % (margin + 1)
    sizes = sizes.at[1:1 + 2 * pairs:2].set(donor - moved).at[2:2 + 2 * pairs:2].set(receiver + moved)
    return sizes[jax.random.permutation(jax.random.fold_in(key, 2), number_of)]


def shared_out(stream_key, own, number, rows, amount, top, limit, slope):
    sequence = jax.random.permutation(stream_key, amount)
    crowded, common = load_shares(amount, rows * top, limit, slope, True), load_shares(amount, rows * top, limit, slope, False)
    places = jnp.arange(amount)

    def named(tallies, turn):
        used = int((tallies > 0).sum())
        fixed = max(1, used // 4)
        passed = fixed + (places - fixed + turn * (used - fixed)) % max(1, amount - fixed)
        return jnp.zeros((amount,), jnp.int32).at[sequence[jnp.where(places < fixed, places, passed)]].set(jnp.asarray(tallies, jnp.int32))

    tallies = jnp.where(number % 4 == 0, named(crowded, number // 4), named(common, number - number // 4 - 1))
    mixed = jax.random.permutation(jax.random.fold_in(own, 3), amount)
    donor, receiver = mixed[0:amount // 2 * 2:2], mixed[1:amount // 2 * 2:2]
    margin = jnp.minimum(tallies[donor] - 1, limit - tallies[receiver]) // 2
    margin = jnp.where((donor == sequence[0]) | (receiver == sequence[0]) | (tallies[receiver] == 0), 0, jnp.maximum(margin, 0))
    passed = jax.random.randint(jax.random.fold_in(own, 4), (amount // 2,), 0, 1 << 20) % (margin + 1)
    tallies = tallies.at[donor].add(-passed).at[receiver].add(passed)
    items = jnp.searchsorted(jnp.cumsum(tallies), jnp.arange(rows * top), side="right").astype(jnp.int32)
    listing = items.reshape(top, rows).T
    listing = listing[jax.random.permutation(jax.random.fold_in(own, 1), rows)]
    turn = jax.random.randint(jax.random.fold_in(own, 2), (rows, 1), 0, top)
    return jnp.take_along_axis(listing, (jnp.arange(top)[None, :] + turn) % top, axis=1)


def load_shares(number_of, total, limit, skew, full):
    portions = [(1 << 20) // math.isqrt(grade ** skew) + 1 for grade in range(1, number_of + 1)]
    largest = limit if full else min(limit, max(-(-total // number_of), total * portions[0] // sum(portions)))
    least = 1 if total - largest >= number_of - 1 else 0
    counts, rest = [largest] + [least] * (number_of - 1), total - largest - least * (number_of - 1)
    while rest > 0:
        candidates = [i for i in range(1, number_of) if counts[i] < largest] or [i for i in range(1, number_of) if counts[i] < limit]
        pool, left = sum([portions[i] for i in candidates]), rest
        for i in candidates:
            more = min(limit - counts[i], max(1, left * portions[i] // pool), rest)
            counts[i] = counts[i] + more
            rest = rest - more
    return np.array(counts)


def centred(rng, dims, scale, most, cuts=(), kind=jnp.bfloat16):
    array = jax.random.normal(rng, dims, jnp.float32) * scale
    if len(cuts) > 0:
        array = shard_levels(rng, dims, cuts, -0.22, 0.18) * array
    return jnp.clip(array, min=-most, max=most).astype(kind)


def setup_inputs(seed: int = 0) -> dict:
    key_list = jax.random.split(jax.random.key(seed), 12)
    kv_cache = draw_kv_cache(jax.random.fold_in(key_list[11], 71), 0)
    query = draw_query(jax.random.fold_in(key_list[11], 71), 0)
    fresh_kv = draw_fresh_kv(jax.random.fold_in(key_list[11], 71), 0)
    lengths = uneven_parts(key_list[3], PROMPT_TOTAL, PROMPT_TOTAL * CACHE_POSITIONS // 2, CACHE_POSITIONS, 2).astype(jnp.int32)
    owner_keys = jax.random.split(jax.random.fold_in(key_list[4], 1), PROMPT_TOTAL // P_DEV)
    owner_turns = jax.random.permutation(jax.random.fold_in(key_list[4], 3), PROMPT_TOTAL // P_DEV)
    owner = jax.vmap(lambda own, number: shared_out(jax.random.fold_in(key_list[4], 2), own, number, P_DEV, N_INST, 1, CAP, 2))(owner_keys, owner_turns).reshape((PROMPT_TOTAL, 1))
    tokens = centred(key_list[5], (MTOK, D), 1.0, 6.0, ((0, 256),))
    expert_ids_keys = jax.random.split(jax.random.fold_in(key_list[6], 1), MTOK // M_DEV)
    expert_ids_turns = jax.random.permutation(jax.random.fold_in(key_list[6], 3), MTOK // M_DEV)
    expert_ids = jax.vmap(lambda own, number: shared_out(jax.random.fold_in(key_list[6], 2), own, number, M_DEV, EXPERTS, TOP, CAPE, 2))(expert_ids_keys, expert_ids_turns).reshape((MTOK, TOP))
    gate_weights = jnp.clip(0.1 + 0.4 * jax.random.uniform(key_list[7], (MTOK, TOP), jnp.float32) ** shard_levels(key_list[7], (MTOK, TOP), ((0, 256),), -0.2, 0.2), 0.1, 0.5)
    w_gate = centred(key_list[8], (EXPERTS * FFE, D), D ** -0.5, 0.09375, ((0, 256),))
    w_up = centred(key_list[9], (EXPERTS * FFE, D), D ** -0.5, 0.09375, ((0, 256),))
    w_down = centred(key_list[10], (EXPERTS * FFE, D), FFE ** -0.5, 0.21875, ((0, 256),))
    return dict(kv_cache=kv_cache, query=query, fresh_kv=fresh_kv, lengths=lengths, owner=owner, tokens=tokens, expert_ids=expert_ids, gate_weights=gate_weights, w_gate=w_gate, w_up=w_up, w_down=w_down)


def slot_index(owner_rows, target, capacity):
    matches_dest = (owner_rows == target).astype(jnp.int32)
    ranking = jnp.cumsum(matches_dest, axis=-1) - 1
    slot_ids = jnp.arange(capacity, dtype=jnp.int32)
    matched = (matches_dest[..., None] == 1) & (ranking[..., None] == slot_ids)
    row_ids = jnp.arange(owner_rows.shape[-1], dtype=jnp.int32)
    chosen = jnp.sum(jnp.where(matched, row_ids[:, None], 0), axis=-2).astype(jnp.int32)
    return chosen, jnp.any(matched, axis=-2)


def to_float(values):
    return lax.optimization_barrier(values.astype(jnp.bfloat16)).astype(jnp.float32)


def decode_attention(query_rows, handed_over, newest_rows, slot_length):
    count_of_slots = query_rows.shape[0]
    prompt_length = handed_over.shape[2]
    query_groups = QUERY_HEADS // KEY_VALUE_HEADS
    score_scale = HEAD_DIM_SIZE ** -0.5
    query_head_count = query_rows.astype(jnp.float32).reshape(count_of_slots, KEY_VALUE_HEADS, query_groups, HEAD_DIM_SIZE)
    every_key = handed_over[:, 0].astype(jnp.float32).reshape(count_of_slots, prompt_length, KEY_VALUE_HEADS, HEAD_DIM_SIZE)
    every_value = handed_over[:, 1].astype(jnp.float32).reshape(count_of_slots, prompt_length, KEY_VALUE_HEADS, HEAD_DIM_SIZE)
    newest_keys = newest_rows[:, :KEY_VALUE_HEADS * HEAD_DIM_SIZE].astype(jnp.float32).reshape(count_of_slots, KEY_VALUE_HEADS, HEAD_DIM_SIZE)
    newest_values = newest_rows[:, KEY_VALUE_HEADS * HEAD_DIM_SIZE:].astype(jnp.float32).reshape(count_of_slots, KEY_VALUE_HEADS, HEAD_DIM_SIZE)
    scores = jnp.einsum("skgd,sjkd->skgj", query_head_count, every_key) * score_scale
    own_score = jnp.einsum("skgd,skd->skg", query_head_count, newest_keys) * score_scale
    live_mask = (jnp.arange(prompt_length)[None, :] < slot_length[:, None])[:, None, None, :]
    highest = jnp.maximum(jnp.max(jnp.where(live_mask, scores, -1e30), axis=-1), own_score)
    exp_terms = jnp.where(live_mask, jnp.exp(scores - highest[..., None]), 0.0)
    own_exp = jnp.exp(own_score - highest)
    totals = jnp.sum(exp_terms, axis=-1) + own_exp
    weights = to_float(exp_terms / totals[..., None])
    own_weight = to_float(own_exp / totals)
    mixed_out = jnp.einsum("skgj,sjkd->skgd", weights, every_value)
    mixed_out = mixed_out + own_weight[..., None] * newest_values[:, :, None, :]
    return mixed_out.reshape(count_of_slots, QUERY_HEADS * HEAD_DIM_SIZE).astype(jnp.bfloat16)


def reference(kv_cache, query, fresh_kv, lengths, owner, tokens, expert_ids, gate_weights, w_gate, w_up, w_down):
    owner_grid = owner[:, 0].reshape(N_INST, P_DEV)
    targets = jnp.arange(N_INST, dtype=jnp.int32)[:, None, None]
    chosen, slot_valid = slot_index(owner_grid[None, :, :], targets, CAP)
    offsets = (jnp.arange(N_INST, dtype=jnp.int32) * P_DEV)[None, :, None]
    slot_prompt = (chosen + offsets).reshape(-1).astype(jnp.int32)
    slot_valid = slot_valid.reshape(-1)
    slot_length = jnp.where(slot_valid, lengths[slot_prompt], 0)
    live_pos = jnp.arange(CACHE_POSITIONS)[None, :] < slot_length[:, None]
    handed_over = jnp.where(live_pos[:, None, :, None], kv_cache[slot_prompt], jnp.zeros((), kv_cache.dtype))
    slot_query = jnp.where(slot_valid[:, None], query[slot_prompt], jnp.zeros((), query.dtype))
    slot_newest = jnp.where(slot_valid[:, None], fresh_kv[slot_prompt], jnp.zeros((), fresh_kv.dtype))
    per_destination = N_INST * CAP

    def attend_block(packed):
        return decode_attention(packed[0], packed[1], packed[2], packed[3])

    attention = lax.map(attend_block, (
        slot_query.reshape(N_INST, per_destination, QUERY_HEADS * HEAD_DIM_SIZE),
        handed_over.reshape(N_INST, per_destination, 2, CACHE_POSITIONS, KEY_VALUE_HEADS * HEAD_DIM_SIZE),
        slot_newest.reshape(N_INST, per_destination, 2 * KEY_VALUE_HEADS * HEAD_DIM_SIZE),
        slot_length.reshape(N_INST, per_destination))).reshape(N_INST * per_destination, QUERY_HEADS * HEAD_DIM_SIZE)

    device_count = N_INST * N_HEAD
    picked_hot = expert_ids[:, :, None] == jnp.arange(EXPERTS, dtype=jnp.int32)[None, None, :]
    counts_hot = jnp.sum(picked_hot.astype(jnp.int32), axis=1)
    gate_table = jnp.sum(jnp.where(picked_hot, gate_weights[:, :, None], 0.0), axis=1)
    blocks = counts_hot.reshape(device_count, M_DEV, EXPERTS)
    ranking = jnp.cumsum(blocks, axis=1) - 1
    slot_ids = jnp.arange(CAPE, dtype=jnp.int32)
    matched = (blocks[..., None] == 1) & (ranking[..., None] == slot_ids)
    token_ids = (jnp.arange(M_DEV, dtype=jnp.int32)[None, :, None, None]
                 + (jnp.arange(device_count, dtype=jnp.int32) * M_DEV)[:, None, None, None])
    pick_rows = jnp.sum(jnp.where(matched, token_ids, 0), axis=1).astype(jnp.int32)
    pick_valid = jnp.any(matched, axis=1)
    pick_rows = jnp.transpose(pick_rows, (1, 0, 2)).reshape(EXPERTS, device_count * CAPE)
    pick_valid = jnp.transpose(pick_valid, (1, 0, 2)).reshape(EXPERTS, device_count * CAPE)
    copies = max(1, N_HEAD // EXP_INST)

    def expert_step(carry, expert):
        rows_here = pick_rows[expert]
        valid_here = pick_valid[expert]
        inputs = jnp.where(valid_here[:, None], tokens[rows_here], jnp.zeros((), tokens.dtype)).astype(jnp.float32)
        start = (expert * FFE).astype(jnp.int32)
        gate_rows = lax.dynamic_slice_in_dim(w_gate, start, FFE, 0).astype(jnp.float32)
        up_rows = lax.dynamic_slice_in_dim(w_up, start, FFE, 0).astype(jnp.float32)
        down_rows = lax.dynamic_slice_in_dim(w_down, start, FFE, 0).astype(jnp.float32)
        gate_val = jnp.dot(inputs, gate_rows.T, preferred_element_type=jnp.float32, precision=lax.Precision.HIGHEST)
        up_val = jnp.dot(inputs, up_rows.T, preferred_element_type=jnp.float32, precision=lax.Precision.HIGHEST)
        hidden = to_float(jax.nn.silu(gate_val) * up_val)
        partial_value = jnp.einsum("rbu,bud->rbd", hidden.reshape(-1, copies, FFE // copies),
                             down_rows.reshape(copies, FFE // copies, D), precision=lax.Precision.HIGHEST)
        expert_out = to_float(jnp.sum(partial_value, axis=1))
        weight_here = jnp.where(valid_here, gate_table[rows_here, expert], 0.0)
        return carry.at[rows_here].add(weight_here[:, None] * expert_out), None

    summed, unused = lax.scan(expert_step, jnp.zeros((MTOK, D), jnp.float32), jnp.arange(EXPERTS, dtype=jnp.int32))
    return handed_over, attention, summed.astype(jnp.bfloat16)
```

```python
import functools

import jax
import jax.numpy as jnp
from jax import lax
from jax.experimental import pallas as pl
from jax.experimental.pallas import tpu as pltpu
from jax.sharding import PartitionSpec as P

MESH = pl.DeviceIdType.MESH
F32 = jnp.float32
BF16 = jnp.bfloat16

D = 4096
UNITS = 384
NCH = 4
DC = D // NCH
TOK = 16
NZ = 8
COL = TOK * NZ
NR = 32
ROWS = NR * TOK
PROMPTS = 24
KVB = 144

STEPS = [
    (1, 0), (3, 0), (0, 1), (0, 3), (1, 1), (3, 3), (1, 3), (3, 1),
    (2, 0), (0, 2), (2, 1), (1, 2), (2, 3), (3, 2), (2, 2),
]
PLANE = [(0, 0, 1)] + [(a, b, 0) for a, b in STEPS] + [(a, b, 1) for a, b in STEPS]
ZSTEPS = (1, 7, 2, 6, 3, 5, 4)


def place():
    i, h = lax.axis_index("inst"), lax.axis_index("head")
    return i // 8, h // 2, lax.rem(i, 8) // 2, lax.rem(h, 2), lax.rem(i, 2)


def device(x, y, z_hi, z_lo, core):
    return (x * 8 + z_hi * 2 + core, y * 2 + z_lo)


def in_plane(dx, dy, dc):
    x, y, zh, zl, c = place()
    return device(lax.rem(x + dx + 4, 4), lax.rem(y + dy + 4, 4), zh, zl, lax.rem(c + dc, 2))


def along_z(dz):
    x, y, zh, zl, c = place()
    z = lax.rem(zh * 2 + zl + dz + 8, 8)
    return device(x, y, z // 2, lax.rem(z, 2), c)


def remote(src, dst, send, recv, dev):
    return pltpu.make_async_remote_copy(
        src_ref=src, dst_ref=dst, send_sem=send, recv_sem=recv, device_id=dev, device_id_type=MESH
    )


def drain(ref, sem):
    pltpu.make_async_copy(ref, ref, sem).wait()


def nt(a, b):
    return lax.dot_general(a, b, (((1,), (1,)), ((), ())), preferred_element_type=F32)


def kernel(
    rows_sm, lens_sm, slot_sm, route, tok, kv, qf, wg_hbm, wu_hbm, wd_hbm,
    hand_hbm, att, moe,
    rbuf, gtok, sel, xin, pout, rin, comb, zin, wg, wu, wd, gacc, uacc, pick, mix,
    kvs, kvr, hand,
    id_s, id_r, zs, zr, xs, xr, rs, rr, cs, cr, ws, ks, ks0, kr, hs,
):
    inst, head = lax.axis_index("inst"), lax.axis_index("head")
    x, y, zh, zl, core = place()
    z = zh * 2 + zl

    barrier = pltpu.get_barrier_semaphore()
    for dx, dy, dc in PLANE:
        pl.semaphore_signal(barrier, inc=1, device_id=in_plane(-dx, -dy, dc), device_id_type=MESH)
    for dz in ZSTEPS:
        pl.semaphore_signal(barrier, inc=1, device_id=along_z(dz), device_id_type=MESH)

    @pl.loop(0, 32)
    def _(t):
        src_i, src_h = head * 4 + t // 8, lax.rem(t, 8)

        @pl.when(jnp.logical_or(src_i != inst, src_h != head))
        def _():
            pl.semaphore_signal(barrier, inc=1, device_id=(src_i, src_h), device_id_type=MESH)

    def weight_copies():
        for n, (src, dst) in enumerate(((wg_hbm, wg), (wu_hbm, wu), (wd_hbm, wd))):
            for c in range(NCH):
                yield pltpu.make_async_copy(src.at[:, pl.ds(c * DC, DC)], dst.at[c], ws.at[n * NCH + c])

    kv_head = inst // 4
    self_kv = kv_head == head
    pl.semaphore_wait(barrier, 31 + 7 + 32 - self_kv.astype(jnp.int32))

    zrows = pl.ds(pl.multiple_of(z * TOK, TOK), TOK)
    pltpu.make_async_copy(route, rbuf.at[z], id_r).start()
    for dz in ZSTEPS:
        remote(route, rbuf.at[z], id_s, id_r, along_z(dz)).start()

    @pl.loop(0, NCH)
    def _(c):
        piece = tok.at[:, pl.ds(pl.multiple_of(c * DC, DC), DC)]
        pltpu.make_async_copy(piece, gtok.at[c, zrows, :], zr.at[c]).start()
        for dz in ZSTEPS:
            remote(piece, gtok.at[c, zrows, :], zs.at[c], zr.at[c], along_z(dz)).start()

    for copy in weight_copies():
        copy.start()

    @pl.loop(0, 64)
    def _(t):
        row, live = rows_sm[t], lens_sm[t]
        mask = lax.broadcasted_iota(jnp.int32, (128, 128), 1) < live
        block = kv[row]
        kvs[t // 2, lax.rem(t, 2), 0:128, :] = jnp.where(mask, block, jnp.zeros_like(block))
        line = qf[row]
        kvs[t // 2, lax.rem(t, 2), 128:144, :] = jnp.where(
            jnp.broadcast_to(live > 0, (16, 128)), line, jnp.zeros_like(line)
        )

    drain(rbuf, id_r)
    routes = jnp.sum(rbuf[...], axis=0)
    r = lax.broadcasted_iota(jnp.int32, (NR, COL), 0)
    ex, ey, ec = lax.rem(x + r // 8, 4), lax.rem(y + lax.rem(r // 2, 4), 4), lax.rem(core + r, 2)
    expert = ((ex * 8 + zh * 2 + ec) * 4 + ey).astype(F32)
    match = jnp.zeros((NR, COL), F32)
    gate = jnp.zeros((NR, COL), F32)
    for k in range(8):
        hit = routes[k : k + 1, :] == expert
        match = match + jnp.where(hit, 1.0, 0.0)
        gate = gate + jnp.where(hit, routes[8 + k : 9 + k, :], 0.0)
    a = lax.broadcasted_iota(jnp.int32, (COL, COL), 0)
    b = lax.broadcasted_iota(jnp.int32, (COL, COL), 1)
    before = jnp.where((a // TOK == b // TOK) & (a < b), 1.0, 0.0).astype(BF16)
    rank = jnp.dot(match.astype(BF16), before, preferred_element_type=F32)
    key = jnp.where(match > 0.0, rank, -1.0)
    wide = lambda v: jnp.broadcast_to(v[:, None, :], (NR, TOK, COL)).reshape(ROWS, COL)
    row = lax.rem(lax.broadcasted_iota(jnp.int32, (ROWS, COL), 0), TOK)
    lane = lax.broadcasted_iota(jnp.int32, (ROWS, COL), 1)
    chosen = (wide(key) == lax.rem(row, 2).astype(F32)) & (lane // TOK == row // 2)
    pick[...] = jnp.where(chosen, 1.0, 0.0).astype(BF16)
    mix[...] = jnp.transpose(jnp.where(chosen, wide(gate), 0.0)).astype(BF16)

    @pl.loop(0, NCH)
    def _(c):
        drain(gtok.at[c], zr.at[c])
        sel[c] = jnp.dot(pick[...], gtok[c], preferred_element_type=F32).astype(BF16)
        pltpu.make_async_copy(sel.at[c, pl.ds(0, TOK)], xin.at[c, pl.ds(0, TOK)], xr.at[c]).start()
        for dx, dy, dc in PLANE:
            block = pl.ds((dx * 8 + dy * 2 + dc) * TOK, TOK)
            remote(sel.at[c, block], xin.at[c, block], xs.at[c], xr.at[c], in_plane(dx, dy, dc)).start()

    mine = lax.rem(inst, 4) * 8 + head

    @pl.when(self_kv)
    def _():
        pltpu.make_async_copy(kvs.at[inst], kvr.at[mine], kr).start()

    @pl.when(jnp.logical_not(self_kv))
    def _():
        remote(kvs.at[inst], kvr.at[mine], ks0, kr, (inst, kv_head)).start()

    @pl.loop(1, 32)
    def _(t):
        dest = lax.rem(x + t // 8, 4) * 8 + lax.rem(zh + lax.rem(t // 2, 4), 4) * 2 + lax.rem(core + t, 2)
        remote(kvs.at[dest], kvr.at[mine], ks, kr, (dest, kv_head)).start()

    for copy in weight_copies():
        copy.wait()
    gacc[...] = jnp.zeros_like(gacc)
    uacc[...] = jnp.zeros_like(uacc)

    @pl.loop(0, NCH)
    def _(c):
        drain(xin.at[c], xr.at[c])
        gacc[...] += nt(xin[c], wg[c])
        uacc[...] += nt(xin[c], wu[c])

    hidden = (gacc[...] / (1.0 + jnp.exp(-gacc[...])) * uacc[...]).astype(BF16)

    @pl.loop(0, NCH)
    def _(c):
        pout[c] = jnp.dot(hidden, wd[c], preferred_element_type=F32).astype(BF16)
        pltpu.make_async_copy(pout.at[c, pl.ds(0, TOK)], rin.at[c, pl.ds(0, TOK)], rr.at[c]).start()
        for dx, dy, dc in PLANE:
            block = pl.ds((dx * 8 + dy * 2 + dc) * TOK, TOK)
            remote(pout.at[c, block], rin.at[c, block], rs.at[c], rr.at[c], in_plane(-dx, -dy, dc)).start()

    drain(kvr, kr)
    a = lax.broadcasted_iota(jnp.int32, (128, 128), 0)
    b = lax.broadcasted_iota(jnp.int32, (128, 128), 1)
    eye = jnp.where(a == b, 1.0, 0.0).astype(BF16)

    @pl.loop(0, 8)
    def _(i):
        s, c = i // 2, lax.rem(i, 2)
        keys = jnp.concatenate([kvr[s * 8 + h, c, 0:64, :] for h in range(8)], axis=0)
        values = jnp.concatenate([kvr[s * 8 + h, c, 64:128, :] for h in range(8)], axis=0)
        lines = [kvr[s * 8 + h, c, 128:144, :].astype(F32) for h in range(8)]
        hand[i, 0] = nt(eye, keys).astype(BF16)
        hand[i, 1] = nt(eye, values).astype(BF16)
        live = lax.broadcasted_iota(jnp.int32, (16, 128), 1) < slot_sm[i]
        for k in range(4):
            q = jnp.concatenate([lines[2 * k][0:8], lines[2 * k + 1][0:8]], axis=0)
            score = jnp.dot(q.astype(BF16), keys[k * 128 : (k + 1) * 128], preferred_element_type=F32) * 128**-0.5
            own = jnp.sum(q * lines[k][8:9], axis=1, keepdims=True) * 128**-0.5
            top = jnp.maximum(jnp.max(jnp.where(live, score, -1e30), axis=1, keepdims=True), own)
            e = jnp.where(live, jnp.exp(score - top), 0.0)
            eo = jnp.exp(own - top)
            total = jnp.sum(e, axis=1, keepdims=True) + eo
            w = (e / total).astype(BF16)
            wo = (eo / total).astype(BF16).astype(F32)
            o = nt(w, values[k * 128 : (k + 1) * 128]) + wo * lines[4 + k][8:9]
            att[i, k * 16 : (k + 1) * 16, :] = o.astype(BF16)

    pltpu.make_async_copy(hand, hand_hbm, hs).start()

    @pl.loop(0, NCH)
    def _(c):
        drain(rin.at[c], rr.at[c])
        comb[c] = jnp.dot(mix[...], rin[c], preferred_element_type=F32).astype(BF16)
        pltpu.make_async_copy(comb.at[c, zrows], zin.at[c, z], cr.at[c]).start()
        for dz in ZSTEPS:
            there = pl.ds(pl.multiple_of(lax.rem(z + dz, 8) * TOK, TOK), TOK)
            remote(comb.at[c, there], zin.at[c, z], cs.at[c], cr.at[c], along_z(dz)).start()

    @pl.loop(0, NCH)
    def _(c):
        drain(zin.at[c], cr.at[c])
        moe[:, pl.ds(pl.multiple_of(c * DC, DC), DC)] = jnp.sum(zin[c].astype(F32), axis=0).astype(BF16)

    drain(rbuf.at[pl.ds(0, 7)], id_s)
    drain(kvs.at[pl.ds(0, 31)], ks)

    @pl.when(jnp.logical_not(self_kv))
    def _():
        drain(kvs.at[0], ks0)

    @pl.loop(0, NCH)
    def _(c):
        drain(gtok.at[c, pl.ds(0, 7 * TOK)], zs.at[c])
        drain(sel.at[c, pl.ds(0, 31 * TOK)], xs.at[c])
        drain(pout.at[c, pl.ds(0, 31 * TOK)], rs.at[c])
        drain(comb.at[c, pl.ds(0, 7 * TOK)], cs.at[c])

    pltpu.make_async_copy(hand, hand_hbm, hs).wait()


def slots(owners, lengths, target):
    p = jnp.arange(PROMPTS, dtype=jnp.int32)
    same = (owners[..., :, None] == owners[..., None, :]) & (p[None, :] < p[:, None])
    rank = jnp.sum(same.astype(jnp.int32), axis=-1)
    hit = (owners[..., None, None, :] == target[..., :, None, None]) & (
        rank[..., None, None, :] == jnp.arange(2, dtype=jnp.int32)[:, None]
    )
    rows = jnp.sum(jnp.where(hit, p, 0), axis=-1)
    lens = jnp.sum(jnp.where(hit, lengths[..., None, None, :], 0), axis=-1)
    return rows, lens


def local(kv_cache, query, fresh_kv, lengths, owner, tokens, expert_ids, gate_weights, w_gate, w_up, w_down):
    inst, head = lax.axis_index("inst"), lax.axis_index("head")
    owners, lens = owner[:, 0].reshape(32, PROMPTS), lengths.reshape(32, PROMPTS)
    own_o = lax.dynamic_index_in_dim(owners, inst, 0, keepdims=False)
    own_l = lax.dynamic_index_in_dim(lens, inst, 0, keepdims=False)
    send_rows, send_lens = slots(own_o, own_l, jnp.arange(32, dtype=jnp.int32))
    src_o = lax.dynamic_slice_in_dim(owners, head * 4, 4, 0)
    src_l = lax.dynamic_slice_in_dim(lens, head * 4, 4, 0)
    _, slot_lens = slots(src_o, src_l, jnp.broadcast_to(inst, (4, 1)))

    z = lax.rem(inst, 8) // 2 * 2 + lax.rem(head, 2)
    route = jnp.concatenate([expert_ids.T.astype(F32), gate_weights.T], axis=0)
    lane = jnp.arange(COL, dtype=jnp.int32)
    route = jnp.where(lane[None, :] // TOK == z, jnp.tile(route, (1, NZ)), 0.0)

    kv = jnp.swapaxes(kv_cache, 2, 3).reshape(PROMPTS, 128, 128)
    qf = jnp.concatenate([query.reshape(PROMPTS, 8, 128), fresh_kv[:, None, :]], axis=1)
    qf = jnp.pad(qf, ((0, 0), (0, 7), (0, 0)))

    vmem, smem, hbm = (pl.BlockSpec(memory_space=s) for s in (pltpu.VMEM, pltpu.SMEM, pl.ANY))
    dma = pltpu.SemaphoreType.DMA
    handed, att, moe = pl.pallas_call(
        kernel,
        out_shape=(
            jax.ShapeDtypeStruct((8, 2, 128, 512), BF16),
            jax.ShapeDtypeStruct((8, 64, 128), BF16),
            jax.ShapeDtypeStruct((TOK, D), BF16),
        ),
        in_specs=[smem] * 3 + [vmem] * 4 + [hbm] * 3,
        out_specs=(hbm, vmem, vmem),
        scratch_shapes=[
            pltpu.VMEM((NZ, 16, COL), F32),
            pltpu.VMEM((NCH, COL, DC), BF16),
            pltpu.VMEM((NCH, ROWS, DC), BF16),
            pltpu.VMEM((NCH, ROWS, DC), BF16),
            pltpu.VMEM((NCH, ROWS, DC), BF16),
            pltpu.VMEM((NCH, ROWS, DC), BF16),
            pltpu.VMEM((NCH, COL, DC), BF16),
            pltpu.VMEM((NCH, NZ, TOK, DC), BF16),
            pltpu.VMEM((NCH, UNITS, DC), BF16),
            pltpu.VMEM((NCH, UNITS, DC), BF16),
            pltpu.VMEM((NCH, UNITS, DC), BF16),
            pltpu.VMEM((ROWS, UNITS), F32),
            pltpu.VMEM((ROWS, UNITS), F32),
            pltpu.VMEM((ROWS, COL), BF16),
            pltpu.VMEM((COL, ROWS), BF16),
            pltpu.VMEM((32, 2, KVB, 128), BF16),
            pltpu.VMEM((32, 2, KVB, 128), BF16),
            pltpu.VMEM((8, 2, 128, 512), BF16),
            dma, dma, dma((NCH,)), dma((NCH,)), dma((NCH,)), dma((NCH,)), dma((NCH,)), dma((NCH,)),
            dma((NCH,)), dma((NCH,)), dma((3 * NCH,)), dma, dma, dma, dma,
        ],
        compiler_params=pltpu.CompilerParams(
            collective_id=1, has_side_effects=True, vmem_limit_bytes=58 * 2**20
        ),
    )(
        send_rows.reshape(64), send_lens.reshape(64), slot_lens.reshape(8), route, tokens, kv, qf,
        w_gate, w_up, w_down,
    )
    return handed, att.reshape(8, 8192), moe


def solution(mesh):
    both = P(("inst", "head"), None)
    in_specs = (
        P("inst", None, None, "head"), P("inst", "head"), P("inst", "head"), P(), P(),
        both, both, both, both, both, both,
    )
    out_specs = (P(("inst", "head"), None, None, None), both, both)
    return jax.shard_map(local, mesh=mesh, in_specs=in_specs, out_specs=out_specs, check_vma=False)
```

```python
import functools

import jax
import jax.numpy as jnp
from jax import lax
from jax.experimental import pallas as pl
from jax.experimental.pallas import tpu as pltpu
from jax.sharding import PartitionSpec as P

MESH = pl.DeviceIdType.MESH
F32 = jnp.float32
BF16 = jnp.bfloat16

D = 4096
UNITS = 384
NCH = 8
DC = D // NCH
NZP = 4
AHEAD = 4
BACK = 4
TURN_Y = (-1, 0)
TURN_Z = (1, 3)
REST = 9
TOK = 16
NZ = 8
COL = TOK * NZ
NR = 32
ROWS = NR * TOK
PROMPTS = 24
KVB = 144

SPREAD = ((0, 1), (1, 0), (3, 0), (2, 0), (1, 1), (3, 1), (2, 1))
PEERS = [(d, 0, c) for d in range(4) for c in range(2) if d + c] + [(0, d, c) for d in (1, 2, 3) for c in range(2)]
ZSTEPS = (1, 7, 2, 6, 3, 5, 4)


def place():
    i, h = lax.axis_index("inst"), lax.axis_index("head")
    return i // 8, h // 2, lax.rem(i, 8) // 2, lax.rem(h, 2), lax.rem(i, 2)


def device(x, y, z_hi, z_lo, core):
    return (x * 8 + z_hi * 2 + core, y * 2 + z_lo)


def in_plane(dx, dy, dc):
    x, y, zh, zl, c = place()
    return device(lax.rem(x + dx + 4, 4), lax.rem(y + dy + 4, 4), zh, zl, lax.rem(c + dc, 2))


def along_z(dz):
    x, y, zh, zl, c = place()
    z = lax.rem(zh * 2 + zl + dz + 8, 8)
    return device(x, y, z // 2, lax.rem(z, 2), c)


def remote(src, dst, send, recv, dev):
    return pltpu.make_async_remote_copy(
        src_ref=src, dst_ref=dst, send_sem=send, recv_sem=recv, device_id=dev, device_id_type=MESH
    )


def drain(ref, sem):
    pltpu.make_async_copy(ref, ref, sem).wait()


def nt(a, b):
    return lax.dot_general(a, b, (((1,), (1,)), ((), ())), preferred_element_type=F32)


def kernel(
    code_sm, route, tok, kv, qf, wg_hbm, wu_hbm, wd_hbm,
    hand_hbm, att, moe,
    rbuf, rcol, xg, sel, xin, pout, rin, pc, via, side, comb, zin, wg, wu, wd, gacc, uacc, pick, mix,
    kvs, kvm, kvy, kvr, hand, heads,
    id_s, id_r, rc_s, rc_r, zs, zr, ds, dr, fs, fr, xs, xr, rs, rr, vs, vr, ss, sr, cs, cr, ws, ks, ks0, kr, ms, mr, ys, yr, hs,
):
    inst, head = lax.axis_index("inst"), lax.axis_index("head")
    x, y, zh, zl, core = place()
    z = zh * 2 + zl

    barrier = pltpu.get_barrier_semaphore()
    for dx, dy, dc in PEERS:
        pl.semaphore_signal(barrier, inc=1, device_id=in_plane(-dx, -dy, dc), device_id_type=MESH)
    for dz in ZSTEPS:
        pl.semaphore_signal(barrier, inc=1, device_id=along_z(dz), device_id_type=MESH)

    for t in range(8):
        src_z = zl * 4 + t // 2
        src_i, src_h = x * 8 + src_z // 2 * 2 + t % 2, y * 2 + lax.rem(src_z, 2)

        @pl.when(jnp.logical_or(src_i != inst, src_h != head))
        def _():
            pl.semaphore_signal(barrier, inc=1, device_id=(src_i, src_h), device_id_type=MESH)

    def weight_copies():
        for n, (src, dst) in enumerate(((wg_hbm, wg), (wu_hbm, wu), (wd_hbm, wd))):
            for c in range(NCH):
                yield pltpu.make_async_copy(src.at[:, pl.ds(c * DC, DC)], dst.at[c], ws.at[n * NCH + c])

    def dense(c, d):
        return in_plane(d, 0, 0) if c % 2 == 0 else in_plane(0, d, 0)

    def spread(c, d, dc):
        return in_plane(0, d, dc) if c % 2 == 0 else in_plane(d, 0, dc)

    def rows_of(ref, c, d, dc):
        return ref.at[c, :, d, dc] if c % 2 == 0 else ref.at[c, d, :, dc]

    near, far = lambda c: (1, 3) if c // 2 % 2 == 0 else (3, 1), 2
    self_kv = zl == zh // 2
    pl.semaphore_wait(barrier, 13 + 7 + 8 - self_kv.astype(jnp.int32))

    zrows = lambda h: pl.ds(pl.multiple_of(lax.rem(z + h + 8, 8) * TOK, TOK), TOK)
    pltpu.make_async_copy(route, rbuf.at[z], id_r).start()
    for dz in ZSTEPS:
        remote(route, rbuf.at[z], id_s, id_r, along_z(dz)).start()
    hops = lambda p: (4, 3) if p % 2 == 0 else (3, 4)
    up, down = along_z(1), along_z(-1)

    def z_block(p, way, h):
        return xg.at[pl.ds(2 * p, 2), 0, zrows(-h if way == 0 else h), :]

    def z_copy(p, way, h):
        block = z_block(p, way, h)
        return remote(block, block, zs.at[p], zr.at[p, way * 4 + h], up if way == 0 else down)

    def z_wait(p, way, h):
        drain(z_block(p, way, h), zr.at[p, way * 4 + h - 1])

    for p in range(NZP):
        for c in (2 * p, 2 * p + 1):
            xg[c, 0, zrows(0), :] = tok[:, c * DC : (c + 1) * DC]
        z_copy(p, 0, 0).start()
        z_copy(p, 1, 0).start()

    for copy in weight_copies():
        copy.start()

    def pack(n):
        @pl.loop(0, 32)
        def _(t):
            code = code_sm[t * 2 + n]
            row, live = code // 256, lax.rem(code, 256)
            mask = lax.broadcasted_iota(jnp.int32, (128, 128), 1) < live
            block = kv[row]
            kvs[n, t, 0:128, :] = jnp.where(mask, block, jnp.zeros_like(block))
            line = qf[row]
            kvs[n, t, 128:144, :] = jnp.where(
                jnp.broadcast_to(live > 0, (16, 128)), line, jnp.zeros_like(line)
            )

        for d in (1, 3, 2):
            there = kvs.at[n, pl.ds(lax.rem(x + d, 4) * 8, 8)]
            remote(there, kvm.at[n, x], ms.at[n], mr.at[n], in_plane(d, 0, 0)).start()
        pltpu.make_async_copy(kvs.at[n, pl.ds(x * 8, 8)], kvm.at[n, x], mr.at[n]).start()

    pack(0)
    for h in (1, 2, 3):
        for p in range(NZP):
            for way in (0, 1):
                z_wait(p, way, h)
                if h < hops(p)[way]:
                    z_copy(p, way, h).start()
        if h == 1:
            pack(1)
        if h == 1:
            drain(rbuf, id_r)
            routes = jnp.sum(rbuf[...], axis=0)
            rcol[0, 0] = routes
            rcol[1, 0] = routes
            for d in (1, 2, 3):
                remote(rcol.at[0, 0], rcol.at[0, d], rc_s.at[0], rc_r.at[0], in_plane(d, 0, 0)).start()
                remote(rcol.at[1, 0], rcol.at[1, d], rc_s.at[1], rc_r.at[1], in_plane(0, d, 0)).start()

    def whole(c):
        if c % 2 == 0:
            z_wait(c // 2, c // 2 % 2, 4)
        for d in near(c):
            remote(xg.at[c, 0], xg.at[c, d], ds.at[c], dr.at[c, d], dense(c, d)).start()

    for c in range(AHEAD):
        whole(c)

    a = lax.broadcasted_iota(jnp.int32, (COL, COL), 0)
    b = lax.broadcasted_iota(jnp.int32, (COL, COL), 1)
    before = jnp.where((a // TOK == b // TOK) & (a < b), 1.0, 0.0).astype(BF16)
    r = lax.rem(lax.broadcasted_iota(jnp.int32, (NR, COL), 0), 8)
    row = lax.rem(lax.broadcasted_iota(jnp.int32, (ROWS, COL), 0), TOK)
    lane = lax.broadcasted_iota(jnp.int32, (ROWS, COL), 1)
    wide = lambda v: jnp.broadcast_to(v[:, None, :], (NR, TOK, COL)).reshape(ROWS, COL)
    for ty in range(2):
        drain(rcol.at[ty, pl.ds(0, 3)], rc_r.at[ty])
        ex = x if ty == 0 else lax.rem(x + r // 2, 4)
        ey = lax.rem(y + r // 2, 4) if ty == 0 else y
        expert = ((ex * 8 + zh * 2 + lax.rem(core + r, 2)) * 4 + ey).astype(F32)
        match = jnp.zeros((NR, COL), F32)
        gate = jnp.zeros((NR, COL), F32)
        for k in range(8):
            line = lambda n: jnp.concatenate(
                [jnp.broadcast_to(rcol[ty, d, n : n + 1, :], (8, COL)) for d in range(4)], axis=0
            )
            hit = line(k) == expert
            match = match + jnp.where(hit, 1.0, 0.0)
            gate = gate + jnp.where(hit, line(8 + k), 0.0)
        rank = jnp.dot(match.astype(BF16), before, preferred_element_type=F32)
        key = jnp.where(match > 0.0, rank, -1.0)
        chosen = (wide(key) == lax.rem(row, 2).astype(F32)) & (lane // TOK == row // 2)
        pick[ty] = jnp.where(chosen, 1.0, 0.0).astype(BF16)
        mix[ty] = jnp.transpose(jnp.where(chosen, wide(gate), 0.0)).astype(BF16)

    def along_y(n):
        drain(kvm.at[n], mr.at[n])
        for d in (1, 3, 2):
            there = kvm.at[n, lax.rem(y + d, 4)]
            remote(there, kvy.at[n, y], ys.at[n], yr.at[n], in_plane(0, d, 0)).start()
        pltpu.make_async_copy(kvm.at[n, y], kvy.at[n, y], yr.at[n]).start()

    def to_owner(n):
        drain(kvy.at[n], yr.at[n])
        mine = kvr.at[n, lax.rem(inst, 4), :, zl]

        def send(t, sem):
            to = lax.rem(zh + t // 2, 4) * 2 + lax.rem(core + t, 2)
            return remote(kvy.at[n, :, to], mine, sem, kr.at[n], (x * 8 + to, y * 2 + zh // 2))

        @pl.when(self_kv)
        def _():
            pltpu.make_async_copy(kvy.at[n, :, zh * 2 + core], mine, kr.at[n]).start()

        @pl.when(jnp.logical_not(self_kv))
        def _():
            send(0, ks0.at[n]).start()

        for t in range(1, 8):
            send(t, ks.at[n]).start()

    for n in range(2):
        if TURN_Y[n] < 0:
            along_y(n)

    def relay(c):
        first, second = near(c)
        drain(xg.at[c, first], dr.at[c, first])
        remote(xg.at[c, first], xg.at[c, far], fs.at[c], fr.at[c], dense(c, first)).start()

    def choose(c):
        first, second = near(c)
        for d in (0, first, second, far):
            if d == second:
                drain(xg.at[c, d], dr.at[c, d])
            if d == far:
                drain(xg.at[c, d], fr.at[c])
            rows = jnp.dot(pick[c % 2, d * 128 : (d + 1) * 128], xg[c, d], preferred_element_type=F32)
            sel[c, d] = rows.astype(BF16).reshape(4, 2, TOK, DC)
        pltpu.make_async_copy(sel.at[c, :, 0, 0], rows_of(xin, c, 0, 0), xr.at[c]).start()
        for d, dc in SPREAD:
            remote(sel.at[c, :, d, dc], rows_of(xin, c, d, dc), xs.at[c], xr.at[c], spread(c, d, dc)).start()

    for t in range(NCH + 1):
        if t < NCH:
            relay(t)
        if t + AHEAD < NCH:
            whole(t + AHEAD)
        if t >= 1:
            choose(t - 1)
        for n in range(2):
            if t == TURN_Y[n]:
                along_y(n)
            if t == TURN_Z[n]:
                to_owner(n)

    for copy in weight_copies():
        copy.wait()
    gacc[...] = jnp.zeros_like(gacc)
    uacc[...] = jnp.zeros_like(uacc)

    @pl.loop(0, NCH)
    def _(c):
        drain(xin.at[c], xr.at[c])
        rows = xin[c].reshape(ROWS, DC)
        gacc[...] += nt(rows, wg[c])
        uacc[...] += nt(rows, wu[c])

    hidden = (gacc[...] / (1.0 + jnp.exp(-gacc[...])) * uacc[...]).astype(BF16)

    def out(c):
        rows = jnp.dot(hidden, wd[c], preferred_element_type=F32)
        pout[c] = rows.astype(BF16).reshape(4, 4, 2, TOK, DC)
        pltpu.make_async_copy(rows_of(pout, c, 0, 0), rin.at[c, :, 0, 0], rr.at[c]).start()
        for d, dc in SPREAD:
            remote(rows_of(pout, c, d, dc), rin.at[c, :, d, dc], rs.at[c], rr.at[c], spread(c, -d, dc)).start()

    for c in range(BACK):
        out(c)

    def attend():
        drain(kvr.at[0], kr.at[0])
        drain(kvr.at[1], kr.at[1])
        a = lax.broadcasted_iota(jnp.int32, (128, 128), 0)
        b = lax.broadcasted_iota(jnp.int32, (128, 128), 1)
        eye = jnp.where(a == b, 1.0, 0.0).astype(BF16)

        @pl.loop(0, 8)
        def _(i):
            s, c = i // 2, lax.rem(i, 2)
            keys = jnp.concatenate([kvr[c, s, h // 2, h % 2, 0:64, :] for h in range(8)], axis=0)
            values = jnp.concatenate([kvr[c, s, h // 2, h % 2, 64:128, :] for h in range(8)], axis=0)
            lines = [kvr[c, s, h // 2, h % 2, 128:144, :].astype(F32) for h in range(8)]
            hand[i, 0] = nt(eye, keys).astype(BF16)
            hand[i, 1] = nt(eye, values).astype(BF16)
            live = lax.broadcasted_iota(jnp.int32, (16, 128), 1) < lax.rem(code_sm[64 + i], 256)
            for k in range(4):
                q = jnp.concatenate([lines[2 * k][0:8], lines[2 * k + 1][0:8]], axis=0)
                score = jnp.dot(q.astype(BF16), keys[k * 128 : (k + 1) * 128], preferred_element_type=F32) * 128**-0.5
                own = jnp.sum(q * lines[k][8:9], axis=1, keepdims=True) * 128**-0.5
                top = jnp.maximum(jnp.max(jnp.where(live, score, -1e30), axis=1, keepdims=True), own)
                e = jnp.where(live, jnp.exp(score - top), 0.0)
                eo = jnp.exp(own - top)
                total = jnp.sum(e, axis=1, keepdims=True) + eo
                w = (e / total).astype(BF16)
                wo = (eo / total).astype(BF16).astype(F32)
                o = nt(w, values[k * 128 : (k + 1) * 128]) + wo * lines[4 + k][8:9]
                heads[i, k * 16 : (k + 1) * 16, :] = o

        pltpu.make_async_copy(hand, hand_hbm, hs).start()

        for q in range(64):
            att[:, q * 128 : (q + 1) * 128] = heads[:, q, :].astype(BF16)

    def sums(c):
        drain(rin.at[c], rr.at[c])
        if c + BACK < NCH:
            out(c + BACK)
        first, second = near(c)
        for d in (far, second, first, 0):
            rows = rin[c, d].reshape(128, DC)
            pc[c, d] = jnp.dot(mix[c % 2, :, d * 128 : (d + 1) * 128], rows, preferred_element_type=F32).astype(BF16)
            if d == far:
                remote(pc.at[c, d], via.at[c], vs.at[c], vr.at[c], dense(c, -first)).start()
            if d == second:
                remote(pc.at[c, d], side.at[c, 1], ss.at[c, 1], sr.at[c, 1], dense(c, -d)).start()

    def passing(c):
        first, second = near(c)
        drain(via.at[c], vr.at[c])
        pc[c, first] = (pc[c, first].astype(F32) + via[c].astype(F32)).astype(BF16)
        remote(pc.at[c, first], side.at[c, 0], ss.at[c, 0], sr.at[c, 0], dense(c, -first)).start()

    def planes(c):
        drain(side.at[c, 1], sr.at[c, 1])
        drain(side.at[c, 0], sr.at[c, 0])
        total = pc[c, 0].astype(F32) + side[c, 0].astype(F32) + side[c, 1].astype(F32)
        comb[c] = total.astype(BF16)
        pltpu.make_async_copy(comb.at[c, zrows(0)], zin.at[c, z], cr.at[c]).start()
        for dz in ZSTEPS:
            remote(comb.at[c, zrows(dz)], zin.at[c, z], cs.at[c], cr.at[c], along_z(dz)).start()

    for t in range(NCH + 2):
        if t < NCH:
            sums(t)
        if 0 <= t - 1 < NCH:
            passing(t - 1)
        if 0 <= t - 2 < NCH:
            planes(t - 2)
        if t == REST:
            attend()

    for c in range(NCH):
        drain(zin.at[c], cr.at[c])
        moe[:, c * DC : (c + 1) * DC] = jnp.sum(zin[c].astype(F32), axis=0).astype(BF16)

    drain(rbuf.at[pl.ds(0, 7)], id_s)
    drain(rcol.at[0, pl.ds(0, 3)], rc_s.at[0])
    drain(rcol.at[1, pl.ds(0, 3)], rc_s.at[1])
    for n in range(2):
        drain(kvm.at[n, pl.ds(0, 3)], ms.at[n])
        drain(kvm.at[n, pl.ds(0, 3)], ys.at[n])
        drain(kvr.at[n, pl.ds(0, 3)], ks.at[n])
        drain(kvr.at[n, 0, pl.ds(0, 2)], ks.at[n])

        @pl.when(jnp.logical_not(self_kv))
        def _():
            drain(kvr.at[n, 0, pl.ds(0, 2)], ks0.at[n])

    for c in range(NCH):
        if c % 2 == 0:
            drain(xg.at[pl.ds(c, 2), 0, pl.ds(0, 7 * TOK)], zs.at[c // 2])
        drain(xg.at[c, pl.ds(0, 2)], ds.at[c])
        drain(xg.at[c, 0], fs.at[c])
        drain(xg.at[c, 0], vs.at[c])
        drain(xg.at[c, 0], ss.at[c, 0])
        drain(xg.at[c, 0], ss.at[c, 1])
        for ref, sem in ((sel, xs), (pout, rs)):
            drain(ref.at[c, pl.ds(0, 3)], sem.at[c])
            drain(ref.at[c, 3, pl.ds(0, 2)], sem.at[c])
        drain(comb.at[c, pl.ds(0, 7 * TOK)], cs.at[c])

    pltpu.make_async_copy(hand, hand_hbm, hs).wait()


def slots(owners, lengths, target):
    p = jnp.arange(PROMPTS, dtype=jnp.int32)
    same = (owners[..., :, None] == owners[..., None, :]) & (p[None, :] < p[:, None])
    rank = jnp.sum(same.astype(jnp.int32), axis=-1)
    hit = (owners[..., None, None, :] == target[..., :, None, None]) & (
        rank[..., None, None, :] == jnp.arange(2, dtype=jnp.int32)[:, None]
    )
    return jnp.sum(jnp.where(hit, (p * 256 + lengths)[..., None, None, :], 0), axis=-1)


def local(kv_cache, query, fresh_kv, lengths, owner, tokens, expert_ids, gate_weights, w_gate, w_up, w_down):
    inst, head = lax.axis_index("inst"), lax.axis_index("head")
    owners, lens = owner[:, 0].reshape(32, PROMPTS), lengths.reshape(32, PROMPTS)
    own_o = lax.dynamic_index_in_dim(owners, inst, 0, keepdims=False)
    own_l = lax.dynamic_index_in_dim(lens, inst, 0, keepdims=False)
    sends = slots(own_o, own_l, jnp.arange(32, dtype=jnp.int32))
    src_o = lax.dynamic_slice_in_dim(owners, head * 4, 4, 0)
    src_l = lax.dynamic_slice_in_dim(lens, head * 4, 4, 0)
    gets = slots(src_o, src_l, jnp.broadcast_to(inst, (4, 1)))
    codes = jnp.concatenate([sends.reshape(64), gets.reshape(8)])

    z = lax.rem(inst, 8) // 2 * 2 + lax.rem(head, 2)
    route = jnp.concatenate([expert_ids.T.astype(F32), gate_weights.T], axis=0)
    lane = jnp.arange(COL, dtype=jnp.int32)
    route = jnp.where(lane[None, :] // TOK == z, jnp.tile(route, (1, NZ)), 0.0)

    kv = jnp.swapaxes(kv_cache, 2, 3).reshape(PROMPTS, 128, 128)
    qf = jnp.concatenate([query.reshape(PROMPTS, 8, 128), fresh_kv[:, None, :]], axis=1)
    qf = jnp.pad(qf, ((0, 0), (0, 7), (0, 0)))

    vmem, smem, hbm = (pl.BlockSpec(memory_space=s) for s in (pltpu.VMEM, pltpu.SMEM, pl.ANY))
    dma = pltpu.SemaphoreType.DMA
    handed, att, moe = pl.pallas_call(
        kernel,
        out_shape=(
            jax.ShapeDtypeStruct((8, 2, 128, 512), BF16),
            jax.ShapeDtypeStruct((8, 64 * 128), BF16),
            jax.ShapeDtypeStruct((TOK, D), BF16),
        ),
        in_specs=[smem] + [vmem] * 4 + [hbm] * 3,
        out_specs=(hbm, vmem, vmem),
        scratch_shapes=[
            pltpu.VMEM((NZ, 16, COL), F32),
            pltpu.VMEM((2, 4, 16, COL), F32),
            pltpu.VMEM((NCH, 4, COL, DC), BF16),
            pltpu.VMEM((NCH, 4, 4, 2, TOK, DC), BF16),
            pltpu.VMEM((NCH, 4, 4, 2, TOK, DC), BF16),
            pltpu.VMEM((NCH, 4, 4, 2, TOK, DC), BF16),
            pltpu.VMEM((NCH, 4, 4, 2, TOK, DC), BF16),
            pltpu.VMEM((NCH, 4, COL, DC), BF16),
            pltpu.VMEM((NCH, COL, DC), BF16),
            pltpu.VMEM((NCH, 2, COL, DC), BF16),
            pltpu.VMEM((NCH, COL, DC), BF16),
            pltpu.VMEM((NCH, NZ, TOK, DC), BF16),
            pltpu.VMEM((NCH, UNITS, DC), BF16),
            pltpu.VMEM((NCH, UNITS, DC), BF16),
            pltpu.VMEM((NCH, UNITS, DC), BF16),
            pltpu.VMEM((ROWS, UNITS), F32),
            pltpu.VMEM((ROWS, UNITS), F32),
            pltpu.VMEM((2, ROWS, COL), BF16),
            pltpu.VMEM((2, COL, ROWS), BF16),
            pltpu.VMEM((2, 32, KVB, 128), BF16),
            pltpu.VMEM((2, 4, 8, KVB, 128), BF16),
            pltpu.VMEM((2, 4, 8, KVB, 128), BF16),
            pltpu.VMEM((2, 4, 4, 2, KVB, 128), BF16),
            pltpu.VMEM((8, 2, 128, 512), BF16),
            pltpu.VMEM((8, 64, 128), F32),
            dma, dma, dma((2,)), dma((2,)), dma((NZP,)), dma((NZP, 8)), dma((NCH,)), dma((NCH, 4)),
            dma((NCH,)), dma((NCH,)), dma((NCH,)), dma((NCH,)), dma((NCH,)), dma((NCH,)),
            dma((NCH,)), dma((NCH,)), dma((NCH, 2)), dma((NCH, 2)), dma((NCH,)), dma((NCH,)),
            dma((3 * NCH,)), dma((2,)), dma((2,)), dma((2,)), dma((2,)), dma((2,)), dma((2,)), dma((2,)), dma,
        ],
        compiler_params=pltpu.CompilerParams(
            collective_id=1, has_side_effects=True, vmem_limit_bytes=58 * 2**20
        ),
    )(
        codes, route, tokens, kv, qf,
        w_gate, w_up, w_down,
    )
    return handed, att, moe


def solution(mesh):
    both = P(("inst", "head"), None)
    in_specs = (
        P("inst", None, None, "head"), P("inst", "head"), P("inst", "head"), P(), P(),
        both, both, both, both, both, both,
    )
    out_specs = (P(("inst", "head"), None, None, None), both, both)
    return jax.shard_map(local, mesh=mesh, in_specs=in_specs, out_specs=out_specs, check_vma=False)
```

```python
import functools

import jax
import jax.numpy as jnp
from jax import lax
from jax.experimental import pallas as pl
from jax.experimental.pallas import tpu as pltpu
from jax.sharding import PartitionSpec as P

MESH = pl.DeviceIdType.MESH
F32 = jnp.float32
BF16 = jnp.bfloat16

D = 4096
UNITS = 384
NCH = 4
DC = D // NCH
NZP = 4
PER = NCH // NZP
AHEAD = 4
BACK = 2
TURN_Y = (-1, 0)
TURN_Z = (1, 2)
REST = 5
TOK = 16
NZ = 8
COL = TOK * NZ
NR = 32
ROWS = NR * TOK
PROMPTS = 24
KVB = 144

SPREAD = ((0, 1), (1, 0), (3, 0), (2, 0), (1, 1), (3, 1), (2, 1))
PEERS = [(d, 0, c) for d in range(4) for c in range(2) if d + c] + [(0, d, c) for d in (1, 2, 3) for c in range(2)]
ZSTEPS = (1, 7, 2, 6, 3, 5, 4)


def place():
    i, h = lax.axis_index("inst"), lax.axis_index("head")
    return i // 8, h // 2, lax.rem(i, 8) // 2, lax.rem(h, 2), lax.rem(i, 2)


def device(x, y, z_hi, z_lo, core):
    return (x * 8 + z_hi * 2 + core, y * 2 + z_lo)


def in_plane(dx, dy, dc):
    x, y, zh, zl, c = place()
    return device(lax.rem(x + dx + 4, 4), lax.rem(y + dy + 4, 4), zh, zl, lax.rem(c + dc, 2))


def along_z(dz):
    x, y, zh, zl, c = place()
    z = lax.rem(zh * 2 + zl + dz + 8, 8)
    return device(x, y, z // 2, lax.rem(z, 2), c)


def remote(src, dst, send, recv, dev):
    return pltpu.make_async_remote_copy(
        src_ref=src, dst_ref=dst, send_sem=send, recv_sem=recv, device_id=dev, device_id_type=MESH
    )


def drain(ref, sem):
    pltpu.make_async_copy(ref, ref, sem).wait()


def nt(a, b):
    return lax.dot_general(a, b, (((1,), (1,)), ((), ())), preferred_element_type=F32)


def kernel(
    code_sm, ids, gates, tok, kv, qf, wg_hbm, wu_hbm, wd_hbm,
    hand_hbm, att, moe,
    route, rbuf, rcol, xg, sel, xin, pout, rin, pc, via, side, comb, zin, wg, wu, wd, gacc, uacc, pick, mix,
    kvs, kvm, kvy, kvr, hand, heads,
    id_s, id_r, rc_s, rc_r, zs, zr, ds, dr, fs, fr, xs, xr, rs, rr, vs, vr, ss, sr, cs, cr, ws, ks, ks0, kr, ms, mr, ys, yr, hs,
):
    inst, head = lax.axis_index("inst"), lax.axis_index("head")
    x, y, zh, zl, core = place()
    z = zh * 2 + zl

    at = lax.broadcasted_iota(jnp.int32, (TOK, COL), 1) - lax.broadcasted_iota(jnp.int32, (TOK, COL), 0)
    spots = jnp.where(at == z * TOK, 1.0, 0.0).astype(BF16)
    for n, part in enumerate((ids, gates)):
        part = part[...].astype(F32).astype(BF16)
        route[n * 8 : (n + 1) * 8, :] = jnp.dot(part, spots, preferred_element_type=F32)

    barrier = pltpu.get_barrier_semaphore()
    for dx, dy, dc in PEERS:
        pl.semaphore_signal(barrier, inc=1, device_id=in_plane(-dx, -dy, dc), device_id_type=MESH)
    for dz in ZSTEPS:
        pl.semaphore_signal(barrier, inc=1, device_id=along_z(dz), device_id_type=MESH)

    for t in range(8):
        src_z = zl * 4 + t // 2
        src_i, src_h = x * 8 + src_z // 2 * 2 + t % 2, y * 2 + lax.rem(src_z, 2)

        @pl.when(jnp.logical_or(src_i != inst, src_h != head))
        def _():
            pl.semaphore_signal(barrier, inc=1, device_id=(src_i, src_h), device_id_type=MESH)

    def weight_copies():
        for n, (src, dst) in enumerate(((wg_hbm, wg), (wu_hbm, wu), (wd_hbm, wd))):
            for c in range(NCH):
                yield pltpu.make_async_copy(src.at[:, pl.ds(c * DC, DC)], dst.at[c], ws.at[n * NCH + c])

    def dense(c, d):
        return in_plane(d, 0, 0) if c % 2 == 0 else in_plane(0, d, 0)

    def spread(c, d, dc):
        return in_plane(0, d, dc) if c % 2 == 0 else in_plane(d, 0, dc)

    def rows_of(ref, c, d, dc):
        return ref.at[c, :, d, dc] if c % 2 == 0 else ref.at[c, d, :, dc]

    near, far = lambda c: (1, 3) if c // 2 % 2 == 0 else (3, 1), 2
    self_kv = zl == zh // 2
    pl.semaphore_wait(barrier, 13 + 7 + 8 - self_kv.astype(jnp.int32))

    zrows = lambda h: pl.ds(pl.multiple_of(lax.rem(z + h + 8, 8) * TOK, TOK), TOK)
    pltpu.make_async_copy(route, rbuf.at[z], id_r).start()
    for dz in ZSTEPS:
        remote(route, rbuf.at[z], id_s, id_r, along_z(dz)).start()
    hops = lambda p: (4, 3) if p % 2 == 0 else (3, 4)
    up, down = along_z(1), along_z(-1)

    def z_block(p, way, h):
        return xg.at[pl.ds(PER * p, PER), 0, zrows(-h if way == 0 else h), :]

    def z_copy(p, way, h):
        block = z_block(p, way, h)
        return remote(block, block, zs.at[p], zr.at[p, way * 4 + h], up if way == 0 else down)

    def z_wait(p, way, h):
        drain(z_block(p, way, h), zr.at[p, way * 4 + h - 1])

    for p in range(NZP):
        for c in range(PER * p, PER * p + PER):
            xg[c, 0, zrows(0), :] = tok[:, c * DC : (c + 1) * DC]
        z_copy(p, 0, 0).start()
        z_copy(p, 1, 0).start()

    for copy in weight_copies():
        copy.start()

    def pack(n):
        @pl.loop(0, 32)
        def _(t):
            code = code_sm[t * 2 + n]
            row, live = code // 256, lax.rem(code, 256)
            mask = lax.broadcasted_iota(jnp.int32, (128, 128), 1) < live
            block = kv[row]
            kvs[n, t, 0:128, :] = jnp.where(mask, block, jnp.zeros_like(block))
            line = qf[row]
            kvs[n, t, 128:144, :] = jnp.where(
                jnp.broadcast_to(live > 0, (16, 128)), line, jnp.zeros_like(line)
            )

        for d in (1, 3, 2):
            there = kvs.at[n, pl.ds(lax.rem(x + d, 4) * 8, 8)]
            remote(there, kvm.at[n, x], ms.at[n], mr.at[n], in_plane(d, 0, 0)).start()
        pltpu.make_async_copy(kvs.at[n, pl.ds(x * 8, 8)], kvm.at[n, x], mr.at[n]).start()

    pack(0)
    for h in (1, 2, 3):
        for p in range(NZP):
            for way in (0, 1):
                z_wait(p, way, h)
                if h < hops(p)[way]:
                    z_copy(p, way, h).start()
        if h == 1:
            pack(1)
        if h == 1:
            drain(rbuf, id_r)
            routes = jnp.sum(rbuf[...], axis=0)
            rcol[0, 0] = routes
            rcol[1, 0] = routes
            for d in (1, 2, 3):
                remote(rcol.at[0, 0], rcol.at[0, d], rc_s.at[0], rc_r.at[0], in_plane(d, 0, 0)).start()
                remote(rcol.at[1, 0], rcol.at[1, d], rc_s.at[1], rc_r.at[1], in_plane(0, d, 0)).start()

    def whole(c):
        if c % PER == 0:
            z_wait(c // PER, c // PER % 2, 4)
        for d in near(c):
            remote(xg.at[c, 0], xg.at[c, d], ds.at[c], dr.at[c, d], dense(c, d)).start()

    for c in range(AHEAD):
        whole(c)

    a = lax.broadcasted_iota(jnp.int32, (COL, COL), 0)
    b = lax.broadcasted_iota(jnp.int32, (COL, COL), 1)
    before = jnp.where((a // TOK == b // TOK) & (a < b), 1.0, 0.0).astype(BF16)
    r = lax.rem(lax.broadcasted_iota(jnp.int32, (NR, COL), 0), 8)
    row = lax.rem(lax.broadcasted_iota(jnp.int32, (ROWS, COL), 0), TOK)
    lane = lax.broadcasted_iota(jnp.int32, (ROWS, COL), 1)
    wide = lambda v: jnp.broadcast_to(v[:, None, :], (NR, TOK, COL)).reshape(ROWS, COL)
    for ty in range(2):
        drain(rcol.at[ty, pl.ds(0, 3)], rc_r.at[ty])
        ex = x if ty == 0 else lax.rem(x + r // 2, 4)
        ey = lax.rem(y + r // 2, 4) if ty == 0 else y
        expert = ((ex * 8 + zh * 2 + lax.rem(core + r, 2)) * 4 + ey).astype(F32)
        match = jnp.zeros((NR, COL), F32)
        gate = jnp.zeros((NR, COL), F32)
        for k in range(8):
            line = lambda n: jnp.concatenate(
                [jnp.broadcast_to(rcol[ty, d, n : n + 1, :], (8, COL)) for d in range(4)], axis=0
            )
            hit = line(k) == expert
            match = match + jnp.where(hit, 1.0, 0.0)
            gate = gate + jnp.where(hit, line(8 + k), 0.0)
        rank = jnp.dot(match.astype(BF16), before, preferred_element_type=F32)
        key = jnp.where(match > 0.0, rank, -1.0)
        chosen = (wide(key) == lax.rem(row, 2).astype(F32)) & (lane // TOK == row // 2)
        pick[ty] = jnp.where(chosen, 1.0, 0.0).astype(BF16)
        mix[ty] = jnp.transpose(jnp.where(chosen, wide(gate), 0.0)).astype(BF16)

    def along_y(n):
        drain(kvm.at[n], mr.at[n])
        for d in (1, 3, 2):
            there = kvm.at[n, lax.rem(y + d, 4)]
            remote(there, kvy.at[n, y], ys.at[n], yr.at[n], in_plane(0, d, 0)).start()
        pltpu.make_async_copy(kvm.at[n, y], kvy.at[n, y], yr.at[n]).start()

    def to_owner(n):
        drain(kvy.at[n], yr.at[n])
        mine = kvr.at[n, lax.rem(inst, 4), :, zl]

        def send(t, sem):
            to = lax.rem(zh + t // 2, 4) * 2 + lax.rem(core + t, 2)
            return remote(kvy.at[n, :, to], mine, sem, kr.at[n], (x * 8 + to, y * 2 + zh // 2))

        @pl.when(self_kv)
        def _():
            pltpu.make_async_copy(kvy.at[n, :, zh * 2 + core], mine, kr.at[n]).start()

        @pl.when(jnp.logical_not(self_kv))
        def _():
            send(0, ks0.at[n]).start()

        for t in range(1, 8):
            send(t, ks.at[n]).start()

    for n in range(2):
        if TURN_Y[n] < 0:
            along_y(n)

    def relay(c):
        first, second = near(c)
        drain(xg.at[c, first], dr.at[c, first])
        remote(xg.at[c, first], xg.at[c, far], fs.at[c], fr.at[c], dense(c, first)).start()

    def choose(c):
        first, second = near(c)
        for d in (0, first, second, far):
            if d == second:
                drain(xg.at[c, d], dr.at[c, d])
            if d == far:
                drain(xg.at[c, d], fr.at[c])
            rows = jnp.dot(pick[c % 2, d * 128 : (d + 1) * 128], xg[c, d], preferred_element_type=F32)
            sel[c, d] = rows.astype(BF16).reshape(4, 2, TOK, DC)
        pltpu.make_async_copy(sel.at[c, :, 0, 0], rows_of(xin, c, 0, 0), xr.at[c]).start()
        for d, dc in SPREAD:
            remote(sel.at[c, :, d, dc], rows_of(xin, c, d, dc), xs.at[c], xr.at[c], spread(c, d, dc)).start()

    for t in range(NCH + 1):
        if t < NCH:
            relay(t)
        if t + AHEAD < NCH:
            whole(t + AHEAD)
        if t >= 1:
            choose(t - 1)
        for n in range(2):
            if t == TURN_Y[n]:
                along_y(n)
            if t == TURN_Z[n]:
                to_owner(n)

    for copy in weight_copies():
        copy.wait()
    gacc[...] = jnp.zeros_like(gacc)
    uacc[...] = jnp.zeros_like(uacc)

    @pl.loop(0, NCH)
    def _(c):
        drain(xin.at[c], xr.at[c])
        rows = xin[c].reshape(ROWS, DC)
        gacc[...] += nt(rows, wg[c])
        uacc[...] += nt(rows, wu[c])

    hidden = (gacc[...] / (1.0 + jnp.exp(-gacc[...])) * uacc[...]).astype(BF16)

    def out(c):
        rows = jnp.dot(hidden, wd[c], preferred_element_type=F32)
        pout[c] = rows.astype(BF16).reshape(4, 4, 2, TOK, DC)
        pltpu.make_async_copy(rows_of(pout, c, 0, 0), rin.at[c, :, 0, 0], rr.at[c]).start()
        for d, dc in SPREAD:
            remote(rows_of(pout, c, d, dc), rin.at[c, :, d, dc], rs.at[c], rr.at[c], spread(c, -d, dc)).start()

    for c in range(BACK):
        out(c)

    def attend():
        drain(kvr.at[0], kr.at[0])
        drain(kvr.at[1], kr.at[1])
        a = lax.broadcasted_iota(jnp.int32, (128, 128), 0)
        b = lax.broadcasted_iota(jnp.int32, (128, 128), 1)
        eye = jnp.where(a == b, 1.0, 0.0).astype(BF16)

        @pl.loop(0, 8)
        def _(i):
            s, c = i // 2, lax.rem(i, 2)
            keys = jnp.concatenate([kvr[c, s, h // 2, h % 2, 0:64, :] for h in range(8)], axis=0)
            values = jnp.concatenate([kvr[c, s, h // 2, h % 2, 64:128, :] for h in range(8)], axis=0)
            lines = [kvr[c, s, h // 2, h % 2, 128:144, :].astype(F32) for h in range(8)]
            hand[i, 0] = nt(eye, keys).astype(BF16)
            hand[i, 1] = nt(eye, values).astype(BF16)
            live = lax.broadcasted_iota(jnp.int32, (16, 128), 1) < lax.rem(code_sm[64 + i], 256)
            for k in range(4):
                q = jnp.concatenate([lines[2 * k][0:8], lines[2 * k + 1][0:8]], axis=0)
                score = jnp.dot(q.astype(BF16), keys[k * 128 : (k + 1) * 128], preferred_element_type=F32) * 128**-0.5
                own = jnp.sum(q * lines[k][8:9], axis=1, keepdims=True) * 128**-0.5
                top = jnp.maximum(jnp.max(jnp.where(live, score, -1e30), axis=1, keepdims=True), own)
                e = jnp.where(live, jnp.exp(score - top), 0.0)
                eo = jnp.exp(own - top)
                total = jnp.sum(e, axis=1, keepdims=True) + eo
                w = (e / total).astype(BF16)
                wo = (eo / total).astype(BF16).astype(F32)
                o = nt(w, values[k * 128 : (k + 1) * 128]) + wo * lines[4 + k][8:9]
                heads[i, k * 16 : (k + 1) * 16, :] = o

        pltpu.make_async_copy(hand, hand_hbm, hs).start()

        for q in range(64):
            att[:, q * 128 : (q + 1) * 128] = heads[:, q, :].astype(BF16)

    def sums(c):
        drain(rin.at[c], rr.at[c])
        if c + BACK < NCH:
            out(c + BACK)
        first, second = near(c)
        for d in (far, second, first, 0):
            rows = rin[c, d].reshape(128, DC)
            pc[c, d] = jnp.dot(mix[c % 2, :, d * 128 : (d + 1) * 128], rows, preferred_element_type=F32).astype(BF16)
            if d == far:
                remote(pc.at[c, d], via.at[c], vs.at[c], vr.at[c], dense(c, -first)).start()
            if d == second:
                remote(pc.at[c, d], side.at[c, 1], ss.at[c, 1], sr.at[c, 1], dense(c, -d)).start()

    def passing(c):
        first, second = near(c)
        drain(via.at[c], vr.at[c])
        pc[c, first] = (pc[c, first].astype(F32) + via[c].astype(F32)).astype(BF16)
        remote(pc.at[c, first], side.at[c, 0], ss.at[c, 0], sr.at[c, 0], dense(c, -first)).start()

    def planes(c):
        drain(side.at[c, 1], sr.at[c, 1])
        drain(side.at[c, 0], sr.at[c, 0])
        total = pc[c, 0].astype(F32) + side[c, 0].astype(F32) + side[c, 1].astype(F32)
        comb[c] = total.astype(BF16)
        pltpu.make_async_copy(comb.at[c, zrows(0)], zin.at[c, z], cr.at[c]).start()
        for dz in ZSTEPS:
            remote(comb.at[c, zrows(dz)], zin.at[c, z], cs.at[c], cr.at[c], along_z(dz)).start()

    for t in range(NCH + 2):
        if t < NCH:
            sums(t)
        if 0 <= t - 1 < NCH:
            passing(t - 1)
        if 0 <= t - 2 < NCH:
            planes(t - 2)
        if t == REST:
            attend()

    for c in range(NCH):
        drain(zin.at[c], cr.at[c])
        moe[:, c * DC : (c + 1) * DC] = jnp.sum(zin[c].astype(F32), axis=0).astype(BF16)

    drain(rbuf.at[pl.ds(0, 7)], id_s)
    drain(rcol.at[0, pl.ds(0, 3)], rc_s.at[0])
    drain(rcol.at[1, pl.ds(0, 3)], rc_s.at[1])
    for n in range(2):
        drain(kvm.at[n, pl.ds(0, 3)], ms.at[n])
        drain(kvm.at[n, pl.ds(0, 3)], ys.at[n])
        drain(kvr.at[n, pl.ds(0, 3)], ks.at[n])
        drain(kvr.at[n, 0, pl.ds(0, 2)], ks.at[n])

        @pl.when(jnp.logical_not(self_kv))
        def _():
            drain(kvr.at[n, 0, pl.ds(0, 2)], ks0.at[n])

    for c in range(NCH):
        if c % PER == 0:
            drain(xg.at[pl.ds(c, PER), 0, pl.ds(0, 7 * TOK)], zs.at[c // PER])
        drain(xg.at[c, pl.ds(0, 2)], ds.at[c])
        drain(xg.at[c, 0], fs.at[c])
        drain(xg.at[c, 0], vs.at[c])
        drain(xg.at[c, 0], ss.at[c, 0])
        drain(xg.at[c, 0], ss.at[c, 1])
        for ref, sem in ((sel, xs), (pout, rs)):
            drain(ref.at[c, pl.ds(0, 3)], sem.at[c])
            drain(ref.at[c, 3, pl.ds(0, 2)], sem.at[c])
        drain(comb.at[c, pl.ds(0, 7 * TOK)], cs.at[c])

    pltpu.make_async_copy(hand, hand_hbm, hs).wait()


def slots(owner, lengths, inst, head):
    take = lambda v: jnp.concatenate(
        [lax.dynamic_slice(v, (inst * PROMPTS,), (PROMPTS,)), lax.dynamic_slice(v, (head * 96,), (96,))]
    )
    who, lens = take(owner.reshape(-1)), take(lengths)
    p, t = jnp.arange(120, dtype=jnp.int32), jnp.arange(72, dtype=jnp.int32)
    group = p // PROMPTS
    rank = jnp.sum(
        ((who[:, None] == who[None, :]) & (group[:, None] == group[None, :]) & (p[None, :] < p[:, None])).astype(jnp.int32),
        axis=1,
    )
    target = jnp.where(t < 64, t // 2, inst)
    part = jnp.where(t < 64, 0, t // 2 - 31)
    hit = (who[None, :] == target[:, None]) & (group[None, :] == part[:, None]) & (rank[None, :] == (t % 2)[:, None])
    return jnp.sum(jnp.where(hit, (p % PROMPTS * 256 + lens)[None, :], 0), axis=1)


def local(kv_cache, query, fresh_kv, lengths, owner, tokens, expert_ids, gate_weights, w_gate, w_up, w_down):
    inst, head = lax.axis_index("inst"), lax.axis_index("head")
    codes = slots(owner, lengths, inst, head)

    kv = jnp.swapaxes(kv_cache, 2, 3).reshape(PROMPTS, 128, 128)
    qf = jnp.concatenate([query.reshape(PROMPTS, 8, 128), fresh_kv[:, None, :]], axis=1)
    qf = jnp.pad(qf, ((0, 0), (0, 7), (0, 0)))

    vmem, smem, hbm = (pl.BlockSpec(memory_space=s) for s in (pltpu.VMEM, pltpu.SMEM, pl.ANY))
    dma = pltpu.SemaphoreType.DMA
    handed, att, moe = pl.pallas_call(
        kernel,
        out_shape=(
            jax.ShapeDtypeStruct((8, 2, 128, 512), BF16),
            jax.ShapeDtypeStruct((8, 64 * 128), BF16),
            jax.ShapeDtypeStruct((TOK, D), BF16),
        ),
        in_specs=[smem] + [vmem] * 5 + [hbm] * 3,
        out_specs=(hbm, vmem, vmem),
        scratch_shapes=[
            pltpu.VMEM((16, COL), F32),
            pltpu.VMEM((NZ, 16, COL), F32),
            pltpu.VMEM((2, 4, 16, COL), F32),
            pltpu.VMEM((NCH, 4, COL, DC), BF16),
            pltpu.VMEM((NCH, 4, 4, 2, TOK, DC), BF16),
            pltpu.VMEM((NCH, 4, 4, 2, TOK, DC), BF16),
            pltpu.VMEM((NCH, 4, 4, 2, TOK, DC), BF16),
            pltpu.VMEM((NCH, 4, 4, 2, TOK, DC), BF16),
            pltpu.VMEM((NCH, 4, COL, DC), BF16),
            pltpu.VMEM((NCH, COL, DC), BF16),
            pltpu.VMEM((NCH, 2, COL, DC), BF16),
            pltpu.VMEM((NCH, COL, DC), BF16),
            pltpu.VMEM((NCH, NZ, TOK, DC), BF16),
            pltpu.VMEM((NCH, UNITS, DC), BF16),
            pltpu.VMEM((NCH, UNITS, DC), BF16),
            pltpu.VMEM((NCH, UNITS, DC), BF16),
            pltpu.VMEM((ROWS, UNITS), F32),
            pltpu.VMEM((ROWS, UNITS), F32),
            pltpu.VMEM((2, ROWS, COL), BF16),
            pltpu.VMEM((2, COL, ROWS), BF16),
            pltpu.VMEM((2, 32, KVB, 128), BF16),
            pltpu.VMEM((2, 4, 8, KVB, 128), BF16),
            pltpu.VMEM((2, 4, 8, KVB, 128), BF16),
            pltpu.VMEM((2, 4, 4, 2, KVB, 128), BF16),
            pltpu.VMEM((8, 2, 128, 512), BF16),
            pltpu.VMEM((8, 64, 128), F32),
            dma, dma, dma((2,)), dma((2,)), dma((NZP,)), dma((NZP, 8)), dma((NCH,)), dma((NCH, 4)),
            dma((NCH,)), dma((NCH,)), dma((NCH,)), dma((NCH,)), dma((NCH,)), dma((NCH,)),
            dma((NCH,)), dma((NCH,)), dma((NCH, 2)), dma((NCH, 2)), dma((NCH,)), dma((NCH,)),
            dma((3 * NCH,)), dma((2,)), dma((2,)), dma((2,)), dma((2,)), dma((2,)), dma((2,)), dma((2,)), dma,
        ],
        compiler_params=pltpu.CompilerParams(
            collective_id=1, has_side_effects=True, vmem_limit_bytes=58 * 2**20
        ),
    )(
        codes, expert_ids.T, gate_weights.T, tokens, kv, qf,
        w_gate, w_up, w_down,
    )
    return handed, att, moe


def solution(mesh):
    both = P(("inst", "head"), None)
    in_specs = (
        P("inst", None, None, "head"), P("inst", "head"), P("inst", "head"), P(), P(),
        both, both, both, both, both, both,
    )
    out_specs = (P(("inst", "head"), None, None, None), both, both)
    return jax.shard_map(local, mesh=mesh, in_specs=in_specs, out_specs=out_specs, check_vma=False)
```
